32 devices in a mesh: leaf: 8 (over y, x, core), front: 4 (over z).
Axes of the slice: x: 2, y: 2, z: 4, core: 2. Of those that a mesh axis runs over, the one named last changes fastest.
Arguments:
- child_pivot: float32 [8, 512, 512], P('leaf', 'front')
- child_panel: float32 [8, 512, 512], P('leaf', 'front'), may hold values from -0.9 to 0.9
- anc_front: float32 [8, 4, 512, 512], P('leaf', 'front')
- dest_list: int32 [8, 4], replicated, may hold values from 0 to 7, as said below
- col_list: int32 [8, 4], replicated, may hold values from 0 to 3, as said below
- row_list: int32 [8, 4], replicated, may hold values from 0 to 3, as said below
Outputs:
- child_lower: float32 [8, 512, 512], P('leaf', 'front')
- child_factor: float32 [8, 512, 512], P('leaf', 'front')
- anc_factor: float32 [8, 4, 512, 512], P('leaf', 'front')
The draws below stay inside these ranges and needn't reach their ends.
Inputs may be any that keep to these rules, and one draw needn't show every extreme that they name: dest_list[g, j] is g with exactly one bit of its index flipped; every group that row g names is named there by exactly 4 column blocks, so row g names 1 different groups. `col_list`: column blocks of one group that name the same group in dest_list have different entries here. row_list[g, f] is 1 or more for f < 4.
All inputs are finite; a program needn't handle non-finite values.
Results may differ from the reference program's by a relative error of at most 0.0001.
Values sent between devices are 32-bit elements; how exact they have to be, the bound alone decides.
A program may use at most 64 MiB of HBM per device.

```python
import math
import jax
import jax.numpy as jnp
from jax import lax

BLK = 128
SCOL = 512
ARB = 4
CB = 4
U = 512
N_LEAF = 8
N_FRONT = 4


def coupled_blocks(key, count):
    keys = jax.random.split(key, 6)
    spacing = float(SCOL) ** (-1.0 / 3.0)
    reach = 0.5 * spacing
    shape = (count, SCOL)
    across = jax.random.uniform(keys[0], shape, jnp.float32)
    along = jax.random.uniform(keys[1], shape, jnp.float32)
    height = jax.random.uniform(keys[2], shape, jnp.float32)
    signs = jnp.where(jax.random.bernoulli(keys[4], 0.5, shape), 1.0, -1.0).astype(jnp.float32)
    scales = jnp.exp(jax.random.uniform(keys[3], shape, jnp.float32, math.log(0.6), math.log(1.6)))
    gap = (across[:, :, None] - across[:, None, :]) ** 2
    gap = gap + (along[:, :, None] - along[:, None, :]) ** 2
    gap = gap + (height[:, :, None] - height[:, None, :]) ** 2
    kernel = jnp.exp(-jnp.sqrt(gap) / reach)
    weights = scales * signs
    coupled = weights[:, :, None] * weights[:, None, :] * kernel
    extra = jax.random.uniform(keys[5], shape, jnp.float32, 0.3, 0.6)
    ids = jnp.arange(SCOL)
    on_diagonal = ids[:, None] == ids[None, :]
    return coupled + jnp.where(on_diagonal[None], extra[:, :, None], 0.0)


def draw_child_pivot(key, part):
    return coupled_blocks(jax.random.fold_in(key, 1), N_LEAF).astype(jnp.float32)


def draw_anc_front(key, part):
    value_key, pivot_key = jax.random.split(jax.random.fold_in(key, 2))
    shape = (N_LEAF, N_FRONT, ARB * BLK, SCOL)
    values = jax.random.normal(value_key, shape, jnp.float32)
    pivot = coupled_blocks(pivot_key, N_LEAF).reshape(N_LEAF, SCOL // BLK, BLK, SCOL)
    return values.at[:, :SCOL // BLK, :BLK, :].set(pivot).astype(jnp.float32)


def shuffle_row(key):
    return jax.random.permutation(key, N_FRONT)


def route_tables(key):
    keys = jax.random.split(jax.random.fold_in(key, 7), 3)
    width_blocks = SCOL // BLK
    named = N_FRONT // width_blocks
    depth = int(N_LEAF).bit_length() - 1
    groups = jnp.arange(N_LEAF, dtype=jnp.int32)
    bit_ids = jnp.arange(depth, dtype=jnp.int32)
    bit_score = jax.random.randint(keys[0], (N_LEAF, depth), 0, 4096) * depth + bit_ids[None, :]
    bits = lax.top_k(bit_score, named)[1].astype(jnp.int32)
    owners = jnp.bitwise_xor(groups[:, None], jnp.left_shift(jnp.ones_like(bits), bits))
    dest = jnp.repeat(owners, width_blocks, axis=1)
    col_ids = jnp.arange(width_blocks, dtype=jnp.int32)
    col_score = jax.random.randint(keys[1], (N_LEAF, named, width_blocks), 0, 4096) * width_blocks + col_ids
    cols = jnp.argsort(col_score, axis=2, stable=True).astype(jnp.int32).reshape(N_LEAF, N_FRONT)
    orders = jax.vmap(shuffle_row)(jax.random.split(keys[2], N_LEAF))
    dest = jnp.take_along_axis(dest, orders, axis=1)
    cols = jnp.take_along_axis(cols, orders, axis=1)
    return (dest.astype(jnp.int32), cols.astype(jnp.int32))


def draw_dest_list(key, part):
    return route_tables(key)[0]


def draw_col_list(key, part):
    return route_tables(key)[1]


def draw_row_list(key, part):
    lowest = (jnp.arange(N_FRONT) < SCOL // BLK).astype(jnp.int32)
    lowest = jnp.broadcast_to(lowest[None, :], (N_LEAF, N_FRONT))
    return jax.random.randint(jax.random.fold_in(key, 9), (N_LEAF, N_FRONT), lowest, ARB).astype(jnp.int32)


def levels(stream_key, extent, pieces, low, largest):
    def one(axis_at, blocks):
        steps = jax.random.uniform(jax.random.fold_in(jax.random.fold_in(stream_key, 6), axis_at), (blocks,), jnp.float32, low / len(pieces), largest / len(pieces))
        return jnp.repeat(jnp.exp(steps), extent[axis_at] // blocks).reshape((-1,) + (1,) * (len(extent) - axis_at - 1))

    gain = one(*pieces[0])
    for cut in pieces[1:]:
        gain = gain * one(*cut)
    return gain


def centred(rng, dims, width, most, shards=(), held_as=jnp.bfloat16):
    drawn = width * jax.random.normal(rng, dims, jnp.float32)
    if shards:
        drawn = drawn * levels(rng, dims, shards, -0.22, 0.18)
    return jnp.clip(drawn, -most, most).astype(held_as)


def setup_inputs(seed: int = 0) -> dict:
    key_list = jax.random.split(jax.random.key(seed), 7)
    child_pivot = draw_child_pivot(jax.random.fold_in(key_list[6], 71), 0)
    child_panel = centred(key_list[1], (N_LEAF, U, SCOL), 0.15, 0.9, ((0, 8), (1, 4)), jnp.float32)
    anc_front = draw_anc_front(jax.random.fold_in(key_list[6], 71), 0)
    dest_list = draw_dest_list(jax.random.fold_in(key_list[6], 71), 0)
    col_list = draw_col_list(jax.random.fold_in(key_list[6], 71), 0)
    row_list = draw_row_list(jax.random.fold_in(key_list[6], 71), 0)
    return dict(child_pivot=child_pivot, child_panel=child_panel, anc_front=anc_front, dest_list=dest_list, col_list=col_list, row_list=row_list)


def place_blocks(acc, update, targets, cols, rows):
    blocks = update.reshape(N_FRONT, BLK, N_FRONT, BLK).transpose(0, 2, 1, 3)
    front_ids = jnp.arange(N_FRONT, dtype=jnp.int32)
    return acc.at[targets[None, :], front_ids[:, None], rows[:, None], :, cols[None, :], :].add(blocks)

def reference(child_pivot, child_panel, anc_front, dest_list, col_list, row_list):

    def child_step(acc, inputs):
        pivot, panel, targets, cols, rows = inputs
        lower = jnp.linalg.cholesky(pivot)
        factor = lax.linalg.triangular_solve(lower, panel, left_side=False, lower=True, transpose_a=True)
        update = jnp.dot(factor.astype(jnp.float32), factor.T.astype(jnp.float32), precision=lax.Precision.HIGHEST, preferred_element_type=jnp.float32)
        acc = place_blocks(acc, update, targets, cols, rows)
        return (acc, (lower, factor))
    start = jnp.zeros((N_LEAF, N_FRONT, ARB, BLK, CB, BLK), jnp.float32)
    received, (child_lower, child_factor) = lax.scan(child_step, start, (child_pivot, child_panel, dest_list, col_list, row_list))
    assembled = anc_front - received.reshape(N_LEAF, N_FRONT, ARB * BLK, SCOL)
    front_ids = jnp.arange(N_FRONT, dtype=jnp.int32)
    row_ids = jnp.arange(ARB * BLK, dtype=jnp.int32)
    mask = (front_ids < CB)[:, None, None] & (row_ids < BLK)[None, :, None]

    def ancestor_step(front):
        pivot = front[:CB, :BLK, :].reshape(SCOL, SCOL)
        lower = jnp.linalg.cholesky(pivot)
        rows_all = front.reshape(N_FRONT * ARB * BLK, SCOL)
        solved = lax.linalg.triangular_solve(lower, rows_all, left_side=False, lower=True, transpose_a=True)
        solved = solved.reshape(N_FRONT, ARB * BLK, SCOL)
        padded = jnp.zeros((N_FRONT, ARB * BLK, SCOL), jnp.float32).at[:CB, :BLK, :].set(lower.reshape(CB, BLK, SCOL))
        return jnp.where(mask, padded, solved)
    anc_factor = lax.map(ancestor_step, assembled)
    return (child_lower, child_factor, anc_factor)
```

```python
import functools

import jax
import jax.numpy as jnp
from jax import lax
from jax.experimental import pallas as pl
from jax.experimental.pallas import tpu as pltpu
from jax.sharding import PartitionSpec as P

T = 128
SUB = 8
VMEM_LIMIT = 56 * 1024 * 1024
MESH = pl.DeviceIdType.MESH


def mm(a, b, dims):
    return lax.dot_general(
        a,
        b,
        (dims, ((), ())),
        precision=lax.Precision.HIGHEST,
        preferred_element_type=jnp.float32,
    )


def mm_nt(a, b):
    return mm(a, b, ((1,), (1,)))


def mm_nn(a, b):
    return mm(a, b, ((1,), (0,)))


def gather_kernel(count, owners, piv, pan, anc, piv_all, pan_all, anc_all, send, recv, local):
    me = lax.axis_index("front")
    barrier = pltpu.get_barrier_semaphore()
    for step in range(1, count):
        other = lax.rem(me + step, count)
        pl.semaphore_signal(barrier, inc=1, device_id={"front": other}, device_id_type=MESH)
    pl.semaphore_wait(barrier, count - 1)
    top = anc.at[pl.ds(0, T)]

    def remote(kind, source, everything, slot, step):
        other = lax.rem(me + step, count)
        return pltpu.make_async_remote_copy(
            src_ref=source,
            dst_ref=everything.at[slot],
            send_sem=send.at[kind, step],
            recv_sem=recv.at[kind, slot],
            device_id={"front": other},
            device_id_type=MESH,
        )

    pairs = ((piv, piv_all), (top, anc_all), (pan, pan_all))

    def when_owner(kind, index, act):
        if kind == 1 and owners < count:
            pl.when(index < owners)(act)
        else:
            act()

    def own_copy(kind):
        source, everything = pairs[kind]
        return pltpu.make_async_copy(source, everything.at[me], local.at[kind])

    for kind in range(3):
        source, everything = pairs[kind]
        for step in range(1, count):

            def start(kind=kind, source=source, everything=everything, step=step):
                remote(kind, source, everything, me, step).start()

            when_owner(kind, me, start)
        when_owner(kind, me, lambda kind=kind: own_copy(kind).start())
    for kind in range(3):
        source, everything = pairs[kind]
        for step in range(1, count):
            sender = lax.rem(me + count - step, count)

            def wait_send(kind=kind, source=source, everything=everything, step=step):
                remote(kind, source, everything, me, step).wait_send()

            def wait_recv(kind=kind, source=source, everything=everything, step=step, sender=sender):
                remote(kind, source, everything, sender, step).wait_recv()

            when_owner(kind, me, wait_send)
            when_owner(kind, sender, wait_recv)
        when_owner(kind, me, lambda kind=kind: own_copy(kind).wait())


def gather_front(piv, pan, anc, count, owners):
    slab, width = piv.shape
    rows = pan.shape[0]
    return pl.pallas_call(
        functools.partial(gather_kernel, count, owners),
        out_shape=(
            jax.ShapeDtypeStruct((count, slab, width), jnp.float32),
            jax.ShapeDtypeStruct((count, rows, width), jnp.float32),
            jax.ShapeDtypeStruct((owners, T, width), jnp.float32),
        ),
        in_specs=[pl.BlockSpec(memory_space=pl.ANY)] * 3,
        out_specs=(pl.BlockSpec(memory_space=pl.ANY),) * 3,
        scratch_shapes=[
            pltpu.SemaphoreType.DMA((3, count)),
            pltpu.SemaphoreType.DMA((3, count)),
            pltpu.SemaphoreType.DMA((3,)),
        ],
        compiler_params=pltpu.CompilerParams(collective_id=0, has_side_effects=True),
        name="gather_front",
    )(piv, pan, anc)


def eliminate(mats):
    lane = lax.broadcasted_iota(jnp.int32, (SUB, T), 1)
    row = lax.broadcasted_iota(jnp.int32, (SUB, T), 0)
    strips = T // SUB
    for p in range(strips):
        for k in range(SUB):
            j = p * SUB + k
            at_j = lane == j
            index = jnp.full((SUB, T), j, jnp.int32)
            for mat in mats:
                cur = mat[p]
                column = jnp.take_along_axis(cur, index, axis=1)
                inverse = 1.0 / jnp.broadcast_to(column[k : k + 1], (SUB, T))
                pivot_row = jnp.broadcast_to(cur[k : k + 1], (SUB, T))
                scaled = jnp.where(at_j, 1.0, pivot_row) * inverse
                if k < SUB - 1:
                    changed = jnp.where(at_j, 0.0, cur) - column * scaled
                    mat[p] = jnp.where(row > k, changed, cur)
                for q in range(p + 1, strips):
                    column = jnp.take_along_axis(mat[q], index, axis=1)
                    mat[q] = jnp.where(at_j, 0.0, mat[q]) - column * scaled


def split_factor(mat):
    full = jnp.concatenate(mat, axis=0)
    lane = lax.broadcasted_iota(jnp.int32, (T, T), 1)
    row = lax.broadcasted_iota(jnp.int32, (T, T), 0)
    diag = lane == row
    pivots = jnp.sum(jnp.where(diag, full, 0.0), axis=1, keepdims=True)
    root = lax.rsqrt(pivots)
    root = root * (1.5 - 0.5 * pivots * root * root)
    upper = jnp.where(lane >= row, full * root, 0.0)
    inverse = jnp.where(diag, root, jnp.where(lane < row, full * root, 0.0))
    return upper, inverse


def factor_kernel(blocks, piv, pan, anc, child_low, child_fac, anc_low, anc_inv, child, front, invs):
    child[...] = piv[...]
    front[...] = anc[...]
    child_fac[...] = pan[...]
    child_low[...] = jnp.zeros_like(child_low)
    anc_low[...] = jnp.zeros_like(anc_low)
    anc_inv[...] = jnp.zeros_like(anc_inv)
    width = blocks * T

    def step(b, carry):
        at = pl.ds(pl.multiple_of(b * T, T), T)
        mats = []
        for ref in (child, front):
            tile = ref[at, at]
            mats.append([tile[s * SUB : (s + 1) * SUB] for s in range(T // SUB)])
        eliminate(mats)
        for which, (mat, low) in enumerate(zip(mats, (child_low, anc_low))):
            upper, inverse = split_factor(mat)
            low[at, at] = upper.T
            invs[which] = inverse
        for c in range(blocks):

            @pl.when(b == c)
            def _(c=c):
                lo, hi = c * T, (c + 1) * T
                inv_c, inv_a = invs[0], invs[1]
                if hi < width:
                    for ref, low, inv in ((child, child_low, inv_c), (front, anc_low, inv_a)):
                        below = mm_nt(ref[hi:, lo:hi], inv)
                        low[hi:, lo:hi] = below
                        ref[hi:, hi:] -= mm_nt(below, below)
                solved = mm_nt(child_fac[:, lo:hi], inv_c)
                child_fac[:, lo:hi] = solved
                if hi < width:
                    child_fac[:, hi:] -= mm_nt(solved, child_low[hi:, lo:hi])
                anc_inv[lo:hi, lo:hi] = inv_a
                if c:
                    crossed = mm_nn(anc_low[lo:hi, :lo], anc_inv[:lo, :lo])
                    anc_inv[lo:hi, :lo] = -mm_nn(inv_a, crossed)

        return carry

    lax.fori_loop(0, blocks, step, 0)


def factor(piv, pan, anc):
    width = piv.shape[1]
    rows = pan.shape[0]
    square = jax.ShapeDtypeStruct((width, width), jnp.float32)
    return pl.pallas_call(
        functools.partial(factor_kernel, width // T),
        out_shape=(square, jax.ShapeDtypeStruct((rows, width), jnp.float32), square, square),
        in_specs=[pl.BlockSpec(memory_space=pltpu.VMEM)] * 3,
        out_specs=(pl.BlockSpec(memory_space=pltpu.VMEM),) * 4,
        scratch_shapes=[
            pltpu.VMEM((width, width), jnp.float32),
            pltpu.VMEM((width, width), jnp.float32),
            pltpu.VMEM((2, T, T), jnp.float32),
        ],
        compiler_params=pltpu.CompilerParams(vmem_limit_bytes=VMEM_LIMIT),
        name="factor",
    )(piv, pan, anc)


def exchange_kernel(levels, fac, arrived, update, send, recv):
    group = lax.axis_index("leaf")
    pos = lax.axis_index("front")
    barrier = pltpu.get_barrier_semaphore()

    def partner(level):
        distance = 1 << level
        up = lax.rem(lax.div(group, distance), 2)
        return group + distance - 2 * distance * up

    for level in range(levels):
        pl.semaphore_signal(
            barrier, inc=1, device_id={"leaf": partner(level)}, device_id_type=MESH
        )
    mine = fac[pl.ds(pl.multiple_of(pos * T, T), T), :]
    update[...] = mm_nt(mine, fac[...])
    pl.semaphore_wait(barrier, levels)
    copies = []
    for level in reversed(range(levels)):
        copy = pltpu.make_async_remote_copy(
            src_ref=update,
            dst_ref=arrived.at[level],
            send_sem=send.at[level],
            recv_sem=recv.at[level],
            device_id={"leaf": partner(level)},
            device_id_type=MESH,
        )
        copy.start()
        copies.append(copy)
    for copy in copies:
        copy.wait()


def exchange(fac, levels):
    rows = fac.shape[0]
    return pl.pallas_call(
        functools.partial(exchange_kernel, levels),
        out_shape=jax.ShapeDtypeStruct((levels, T, rows), jnp.float32),
        in_specs=[pl.BlockSpec(memory_space=pltpu.VMEM)],
        out_specs=pl.BlockSpec(memory_space=pltpu.VMEM),
        scratch_shapes=[
            pltpu.VMEM((T, rows), jnp.float32),
            pltpu.SemaphoreType.DMA((levels,)),
            pltpu.SemaphoreType.DMA((levels,)),
        ],
        compiler_params=pltpu.CompilerParams(
            collective_id=1, has_side_effects=True, vmem_limit_bytes=VMEM_LIMIT
        ),
        name="exchange",
    )(fac)


def finish_kernel(
    blocks, levels, count, dest, cols, rows, anc, arrived, anc_inv, anc_low, child_low, fac,
    out_low, out_fac, out_anc,
):
    group = lax.axis_index("leaf")
    pos = lax.axis_index("front")
    slab = out_low.shape[0]
    out_low[...] = child_low[pl.ds(pl.multiple_of(pos * slab, slab), slab), :]
    out_fac[...] = fac[pl.ds(pl.multiple_of(pos * T, T), T), :]
    out_anc[...] = anc[...]
    for level in range(levels):
        distance = 1 << level
        up = lax.rem(lax.div(group, distance), 2)
        sender = group + distance - 2 * distance * up
        slot = rows[sender, pos]
        at = pl.ds(pl.multiple_of(slot * T, T), T)
        for j in range(count):

            @pl.when(dest[sender, j] == group)
            def _(level=level, j=j, sender=sender, at=at):
                where = pl.ds(pl.multiple_of(cols[sender, j] * T, T), T)
                out_anc[at, where] -= arrived[level, :, j * T : (j + 1) * T]

    inv = anc_inv
    for c in reversed(range(blocks)):
        hi = (c + 1) * T
        out_anc[:, c * T : hi] = mm_nt(out_anc[:, :hi], inv[c * T : hi, :hi])

    @pl.when(pos < blocks)
    def _():
        first = jnp.minimum(pos, blocks - 1)
        out_anc[:T, :] = anc_low[pl.ds(pl.multiple_of(first * T, T), T), :]


def finish(dest, cols, rows, anc, arrived, anc_inv, anc_low, child_low, fac, slab, levels, count):
    width = anc.shape[1]
    smem = pl.BlockSpec(memory_space=pltpu.SMEM)
    vmem = pl.BlockSpec(memory_space=pltpu.VMEM)
    return pl.pallas_call(
        functools.partial(finish_kernel, width // T, levels, count),
        out_shape=(
            jax.ShapeDtypeStruct((slab, width), jnp.float32),
            jax.ShapeDtypeStruct((T, width), jnp.float32),
            jax.ShapeDtypeStruct(anc.shape, jnp.float32),
        ),
        in_specs=[smem] * 3 + [vmem] * 6,
        out_specs=(vmem,) * 3,
        compiler_params=pltpu.CompilerParams(vmem_limit_bytes=VMEM_LIMIT),
        name="finish",
    )(dest, cols, rows, anc, arrived, anc_inv, anc_low, child_low, fac)


def per_device(child_pivot, child_panel, anc_front, dest_list, col_list, row_list):
    count = lax.axis_size("front")
    levels = lax.axis_size("leaf").bit_length() - 1
    slab, width = child_pivot.shape[1:]
    anc = anc_front[0, 0]
    piv_all, pan_all, anc_all = gather_front(
        child_pivot[0], child_panel[0], anc, count, width // T
    )
    child_low, fac, anc_low, anc_inv = factor(
        piv_all.reshape(width, width),
        pan_all.reshape(count * T, width),
        anc_all.reshape(width, width),
    )
    arrived = exchange(fac, levels)
    low, own, out = finish(
        dest_list, col_list, row_list, anc, arrived, anc_inv, anc_low, child_low, fac,
        slab, levels, count,
    )
    return (low[None], own[None], out[None, None])


def solution(mesh):
    in_specs = (
        P("leaf", "front", None),
        P("leaf", "front", None),
        P("leaf", "front", None, None),
        P(),
        P(),
        P(),
    )
    out_specs = (P("leaf", "front", None), P("leaf", "front", None), P("leaf", "front", None, None))
    return jax.shard_map(
        per_device, mesh=mesh, in_specs=in_specs, out_specs=out_specs, check_vma=False
    )
```

```python
import functools

import jax
import jax.numpy as jnp
from jax import lax
from jax.experimental import pallas as pl
from jax.experimental.pallas import tpu as pltpu
from jax.sharding import PartitionSpec as P

T = 128
SUB = 8
VMEM_LIMIT = 56 * 1024 * 1024
MESH = pl.DeviceIdType.MESH


def mm(a, b, dims):
    return lax.dot_general(
        a,
        b,
        (dims, ((), ())),
        precision=lax.Precision.HIGHEST,
        preferred_element_type=jnp.float32,
    )


def mm_nt(a, b):
    return mm(a, b, ((1,), (1,)))


def mm_nn(a, b):
    return mm(a, b, ((1,), (0,)))


def routes(count):
    found = []
    for i in range(count):
        for j in range(i, count):
            for k in range(count):
                if k in (i, j):
                    continue
                near_i, near_j = abs(i - k), abs(j - k)
                first = near_i < near_j or (near_i == near_j and 2 * k < count)
                found.append((i, j, k) if first else (j, i, k))
    found.sort(key=lambda r: (min(r[0], r[1]), -abs(r[0] - r[2])))
    return found


def partner_of(group, level):
    distance = 1 << level
    up = lax.rem(lax.div(group, distance), 2)
    return group + distance - 2 * distance * up


def eliminate(mats):
    lane = lax.broadcasted_iota(jnp.int32, (SUB, T), 1)
    row = lax.broadcasted_iota(jnp.int32, (SUB, T), 0)
    strips = T // SUB
    done = [[] for _ in mats]
    rest = list(mats)
    for p in range(strips):
        base = p * SUB
        inside = (lane >= base) & (lane < base + SUB)
        for w in range(len(mats)):
            below = rest[w]
            high = below.shape[0]
            columns = [
                jnp.take_along_axis(below, jnp.full((high, T), base + m, jnp.int32), axis=1)
                for m in range(SUB)
            ]
            own = jnp.stack([column[:SUB] for column in columns], axis=0)
            reduced = below[:SUB]
            full = jnp.where(inside, jnp.where(lane == base + row, 1.0, 0.0), reduced)
            kept_reduced, kept_full = reduced, full
            for k in range(SUB):
                pivots = jnp.broadcast_to(own[:, k : k + 1], (SUB, SUB, T))
                inverse = 1.0 / pivots[k]
                factor = jnp.where(row == k, 0.0, own[k]) * inverse
                row_full = jnp.broadcast_to(full[k : k + 1], (SUB, T))
                row_reduced = jnp.broadcast_to(reduced[k : k + 1], (SUB, T))
                kept_full = jnp.where(row == k, row_full, kept_full)
                kept_reduced = jnp.where(row == k, row_reduced, kept_reduced)
                if k < SUB - 1:
                    own = own - factor[None] * pivots
                    reduced = reduced - factor * row_reduced
                full = full - factor * row_full
                scale = inverse if k == 0 else jnp.where(row == k, inverse, scale)
            full = full * scale
            done[w].append(jnp.where(lane < base + row, kept_full, kept_reduced))
            if p < strips - 1:
                left = high - SUB
                inside_left = jnp.broadcast_to(inside[:1], (left, T))
                terms = [
                    columns[m][SUB:] * jnp.broadcast_to(full[m : m + 1], (left, T))
                    for m in range(SUB)
                ]
                while len(terms) > 1:
                    terms = [terms[i] + terms[i + 1] for i in range(0, len(terms), 2)]
                rest[w] = jnp.where(inside_left, 0.0, below[SUB:]) - terms[0]
    return [jnp.concatenate(strip, axis=0) for strip in done]


def split_factor(full):
    lane = lax.broadcasted_iota(jnp.int32, (T, T), 1)
    row = lax.broadcasted_iota(jnp.int32, (T, T), 0)
    diag = lane == row
    pivots = jnp.sum(jnp.where(diag, full, 0.0), axis=1, keepdims=True)
    root = lax.rsqrt(pivots)
    root = root * (1.5 - 0.5 * pivots * root * root)
    upper = jnp.where(lane >= row, full * root, 0.0)
    inverse = jnp.where(diag, root, jnp.where(lane < row, full * root, 0.0))
    return upper, inverse


def front_kernel(
    blocks, count, levels, piv, pan, anc, arrived, own_low, own_fac, anc_low, anc_inv,
    child, front, panels, child_low, child_inv, invs, update,
    send, recv, pan_send, pan_recv, local, up_send, up_recv,
):
    me = lax.axis_index("front")
    group = lax.axis_index("leaf")
    slab, width = piv.shape
    tiled = count == blocks
    mats = ((piv, child), (anc, front))

    barrier = pltpu.get_barrier_semaphore()
    for step in range(1, count):
        other = lax.rem(me + step, count)
        pl.semaphore_signal(barrier, inc=1, device_id={"front": other}, device_id_type=MESH)
    for level in range(levels):
        partner = partner_of(group, level)
        pl.semaphore_signal(barrier, inc=1, device_id={"leaf": partner}, device_id_type=MESH)
    pl.semaphore_wait(barrier, count - 1 + levels)

    def tile_copy(which, source, column, target, slot):
        src, dst = mats[which]
        return pltpu.make_async_remote_copy(
            src_ref=src.at[pl.ds(0, T), pl.ds(column * T, T)],
            dst_ref=dst.at[pl.ds(source * T, T), pl.ds(column * T, T)],
            send_sem=send.at[which, slot],
            recv_sem=recv.at[which, source * blocks + column],
            device_id={"front": jnp.int32(target)},
            device_id_type=MESH,
        )

    def row_copy(which, slot, step):
        src, dst = mats[which]
        high = (slab, T)[which]
        return pltpu.make_async_remote_copy(
            src_ref=src.at[pl.ds(0, high)],
            dst_ref=dst.at[pl.ds(pl.multiple_of(slot * high, high), high)],
            send_sem=send.at[which, step],
            recv_sem=recv.at[which, slot],
            device_id={"front": lax.rem(me + step, count)},
            device_id_type=MESH,
        )

    def panel_copy(slot, step):
        return pltpu.make_async_remote_copy(
            src_ref=pan,
            dst_ref=panels.at[pl.ds(pl.multiple_of(slot * T, T), T)],
            send_sem=pan_send.at[step],
            recv_sem=pan_recv.at[slot],
            device_id={"front": lax.rem(me + step, count)},
            device_id_type=MESH,
        )

    def own_copy(which):
        if which == 2:
            src, dst, high = pan, panels, T
        else:
            (src, dst), high = mats[which], (slab, T)[which]
        return pltpu.make_async_copy(
            src.at[pl.ds(0, high)],
            dst.at[pl.ds(pl.multiple_of(me * high, high), high)],
            local.at[which],
        )

    def on_owner(which, index, act):
        if which == 1 and blocks < count:
            pl.when(index < blocks)(act)
        else:
            act()

    plan = routes(count) if tiled else []
    for which in range(2):
        on_owner(which, me, lambda which=which: own_copy(which).start())
    own_copy(2).start()
    if tiled:
        for source in range(count):

            @pl.when(me == source)
            def _(source=source):
                mine = [r for r in plan if r[0] == source]
                for slot, (_, column, target) in enumerate(mine):
                    for which in range(2):
                        tile_copy(which, source, column, target, slot).start()

    else:
        for which in range(2):
            for step in range(1, count):
                on_owner(which, me, lambda w=which, s=step: row_copy(w, me, s).start())
    for step in range(1, count):
        panel_copy(me, step).start()

    for which in range(2):
        on_owner(which, me, lambda which=which: own_copy(which).wait())
    own_copy(2).wait()

    def wait_tiles(first):
        for target in range(count):

            @pl.when(me == target)
            def _(target=target):
                for source, column, to in plan:
                    if to == target and (source == column == 0) == first:
                        for which in range(2):
                            tile_copy(which, source, column, to, 0).wait_recv()
                if not first:
                    for high in range(count):
                        for low in range(high):
                            lower = high == target or (high, low, target) in plan
                            if not lower:
                                for _, dst in mats:
                                    flip = dst[low * T : (low + 1) * T, high * T : (high + 1) * T]
                                    dst[high * T : (high + 1) * T, low * T : (low + 1) * T] = flip.T

    if tiled:
        wait_tiles(True)
    else:
        for which in range(2):
            for step in range(1, count):
                sender = lax.rem(me + count - step, count)
                on_owner(
                    which, sender, lambda w=which, f=sender, s=step: row_copy(w, f, s).wait_recv()
                )

    child_low[...] = jnp.zeros_like(child_low)
    anc_low[...] = jnp.zeros_like(anc_low)
    child_inv[...] = jnp.zeros_like(child_inv)
    anc_inv[...] = jnp.zeros_like(anc_inv)

    def step(b, carry):
        at = pl.ds(pl.multiple_of(b * T, T), T)
        packed = eliminate([child[at, at], front[at, at]])
        for which, low in enumerate((child_low, anc_low)):
            upper, inverse = split_factor(packed[which])
            low[at, at] = upper.T
            invs[which] = inverse
        for c in range(blocks):

            @pl.when(b == c)
            def _(c=c):
                if c == 0 and tiled:
                    wait_tiles(False)
                lo, hi = c * T, (c + 1) * T
                both = ((child, child_low, child_inv), (front, anc_low, anc_inv))
                for which, (ref, low, inv) in enumerate(both):
                    tile_inv = invs[which]
                    if hi < width:
                        low[hi:, lo:hi] = mm_nt(ref[hi:, lo:hi], tile_inv)
                        for j in range(hi, width, T):
                            ref[j:, j : j + T] -= mm_nt(low[j:, lo:hi], low[j : j + T, lo:hi])
                    inv[lo:hi, lo:hi] = tile_inv
                    if c:
                        crossed = mm_nn(low[lo:hi, :lo], inv[:lo, :lo])
                        inv[lo:hi, :lo] = -mm_nn(tile_inv, crossed)

        return carry

    lax.fori_loop(0, blocks, step, 0)

    for step_back in range(1, count):
        sender = lax.rem(me + count - step_back, count)
        panel_copy(sender, step_back).wait_recv()
    for c in reversed(range(blocks)):
        hi = (c + 1) * T
        panels[:, c * T : hi] = mm_nt(panels[:, :hi], child_inv[c * T : hi, :hi])
    own_fac[...] = panels[pl.ds(pl.multiple_of(me * T, T), T), :]
    update[...] = mm_nt(own_fac[...], panels[...])
    copies = []
    for level in reversed(range(levels)):
        copy = pltpu.make_async_remote_copy(
            src_ref=update,
            dst_ref=arrived.at[level],
            send_sem=up_send.at[level],
            recv_sem=up_recv.at[level],
            device_id={"leaf": partner_of(group, level)},
            device_id_type=MESH,
        )
        copy.start()
        copies.append(copy)
    own_low[...] = child_low[pl.ds(pl.multiple_of(me * slab, slab), slab), :]
    if tiled:
        for source in range(count):

            @pl.when(me == source)
            def _(source=source):
                mine = [r for r in plan if r[0] == source]
                for slot, (_, column, target) in enumerate(mine):
                    for which in range(2):
                        tile_copy(which, source, column, target, slot).wait_send()

    else:
        for which in range(2):
            for step_on in range(1, count):
                on_owner(which, me, lambda w=which, s=step_on: row_copy(w, me, s).wait_send())
    for step_on in range(1, count):
        panel_copy(me, step_on).wait_send()
    for copy in copies:
        copy.wait()


def fronts(piv, pan, anc, count, levels):
    slab, width = piv.shape
    blocks = width // T
    slots = max(count, 2 * blocks)
    square = jax.ShapeDtypeStruct((width, width), jnp.float32)
    square_scratch = pltpu.VMEM((width, width), jnp.float32)
    vmem = pl.BlockSpec(memory_space=pltpu.VMEM)
    dma = pltpu.SemaphoreType.DMA
    return pl.pallas_call(
        functools.partial(front_kernel, blocks, count, levels),
        out_shape=(
            jax.ShapeDtypeStruct((levels, T, count * T), jnp.float32),
            jax.ShapeDtypeStruct((slab, width), jnp.float32),
            jax.ShapeDtypeStruct((T, width), jnp.float32),
            square,
            square,
        ),
        in_specs=[pl.BlockSpec(memory_space=pl.ANY)] * 3,
        out_specs=(vmem,) * 5,
        scratch_shapes=[
            square_scratch,
            square_scratch,
            pltpu.VMEM((count * T, width), jnp.float32),
            square_scratch,
            square_scratch,
            pltpu.VMEM((2, T, T), jnp.float32),
            pltpu.VMEM((T, count * T), jnp.float32),
            dma((2, slots)),
            dma((2, max(count, blocks * blocks))),
            dma((count,)),
            dma((count,)),
            dma((3,)),
            dma((levels,)),
            dma((levels,)),
        ],
        compiler_params=pltpu.CompilerParams(
            collective_id=0, has_side_effects=True, vmem_limit_bytes=VMEM_LIMIT
        ),
        name="fronts",
    )(piv, pan, anc)


def finish_kernel(
    blocks, levels, count, tables, anc, arrived, anc_inv, anc_low, own_low, own_fac,
    out_low, out_fac, out_anc,
):
    group = lax.axis_index("leaf")
    pos = lax.axis_index("front")
    out_low[...] = own_low[...]
    out_fac[...] = own_fac[...]
    out_anc[...] = anc[...]
    for level in range(levels):
        sender = partner_of(group, level)
        slot = tables[2, sender, pos]
        at = pl.ds(pl.multiple_of(slot * T, T), T)
        for j in range(count):

            @pl.when(tables[0, sender, j] == group)
            def _(level=level, j=j, sender=sender, at=at):
                where = pl.ds(pl.multiple_of(tables[1, sender, j] * T, T), T)
                out_anc[at, where] -= arrived[level, :, j * T : (j + 1) * T]

    inv = anc_inv
    for c in reversed(range(blocks)):
        hi = (c + 1) * T
        out_anc[:, c * T : hi] = mm_nt(out_anc[:, :hi], inv[c * T : hi, :hi])

    @pl.when(pos < blocks)
    def _():
        first = jnp.minimum(pos, blocks - 1)
        out_anc[:T, :] = anc_low[pl.ds(pl.multiple_of(first * T, T), T), :]


def finish(tables, anc, arrived, anc_inv, anc_low, own_low, own_fac, levels, count):
    width = anc.shape[1]
    smem = pl.BlockSpec(memory_space=pltpu.SMEM)
    vmem = pl.BlockSpec(memory_space=pltpu.VMEM)
    return pl.pallas_call(
        functools.partial(finish_kernel, width // T, levels, count),
        out_shape=(
            jax.ShapeDtypeStruct(own_low.shape, jnp.float32),
            jax.ShapeDtypeStruct(own_fac.shape, jnp.float32),
            jax.ShapeDtypeStruct(anc.shape, jnp.float32),
        ),
        in_specs=[smem] + [vmem] * 6,
        out_specs=(vmem,) * 3,
        compiler_params=pltpu.CompilerParams(vmem_limit_bytes=VMEM_LIMIT),
        name="finish",
    )(tables, anc, arrived, anc_inv, anc_low, own_low, own_fac)


def per_device(child_pivot, child_panel, anc_front, dest_list, col_list, row_list):
    count = lax.axis_size("front")
    levels = lax.axis_size("leaf").bit_length() - 1
    anc = anc_front[0, 0]
    arrived, own_low, own_fac, anc_low, anc_inv = fronts(
        child_pivot[0], child_panel[0], anc, count, levels
    )
    tables = jnp.stack([dest_list, col_list, row_list])
    low, own, out = finish(
        tables, anc, arrived, anc_inv, anc_low, own_low, own_fac, levels, count
    )
    return (low[None], own[None], out[None, None])


def solution(mesh):
    in_specs = (
        P("leaf", "front", None),
        P("leaf", "front", None),
        P("leaf", "front", None, None),
        P(),
        P(),
        P(),
    )
    out_specs = (P("leaf", "front", None), P("leaf", "front", None), P("leaf", "front", None, None))
    return jax.shard_map(
        per_device, mesh=mesh, in_specs=in_specs, out_specs=out_specs, check_vma=False
    )
```
